512 devices in a mesh: gx: 8 (over z_lo, core), gy: 8 (over x, z_hi), gz: 8 (over y).
Axes of the slice: x: 4, y: 8, z: 8 (z_hi: 2, z_lo: 4; z = z_hi * 4 + z_lo), core: 2. Of those that a mesh axis runs over, the one named last changes fastest.
Arguments:
- tokens: bfloat16 [1024, 8192], P('gx', ('gz', 'gy')), may hold values from -6 to 6
- gate_weight: bfloat16 [8192, 16384], P('gz', ('gy', 'gx')), may hold values from -0.0625 to 0.0625
- up_weight: bfloat16 [8192, 16384], P('gz', ('gy', 'gx')), may hold values from -0.0625 to 0.0625
- hidden_grad: bfloat16 [1024, 16384], P('gx', ('gy', 'gz')), may hold values from -1.5 to 1.5
Outputs:
- hidden: bfloat16 [1024, 16384], P('gx', ('gy', 'gz'))
- input_grad: bfloat16 [1024, 8192], P('gx', ('gz', 'gy'))
- gate_wgrad: bfloat16 [8192, 16384], P('gz', ('gy', 'gx'))
- up_wgrad: bfloat16 [8192, 16384], P('gz', ('gy', 'gx'))
The draws below stay inside these ranges and needn't reach their ends.
All inputs are finite; a program needn't handle non-finite values.
Results may differ from the reference program's by a relative error of at most 0.005.
Values may be sent and summed in bfloat16 or wider, within the bound.
No kernel may reach another device: no remote copies, remote signals or barrier semaphores. Data moves between devices by JAX's collectives and lax.ppermute only.
A program may use at most 64 MiB of HBM per device.

```python
import jax
import jax.numpy as jnp
from jax import lax

D = 8192
FF = 16384
TOKENS = 1024


def block_levels(rng, extent, cuts, least, high):
    level, own = 1.0, jax.random.fold_in(rng, 6)
    for axis_at, parts in cuts:
        heights = jnp.exp(jax.random.uniform(jax.random.fold_in(own, axis_at), (parts,), jnp.float32, least / len(cuts), high / len(cuts)))
        level = level * jnp.repeat(heights, extent[axis_at] // parts).reshape([-1 if axis == axis_at else 1 for axis in range(len(extent))])
    return level


def noise(stream_key, extent, deviation, bound, cuts=(), dtype=jnp.bfloat16):
    entries = deviation * jax.random.normal(stream_key, extent, jnp.float32)
    if cuts:
        entries = entries * block_levels(stream_key, extent, cuts, -0.22, 0.18)
    return jnp.clip(entries, -bound, bound).astype(dtype)


def setup_inputs(seed: int = 0) -> dict:
    streams_of = jax.random.split(jax.random.key(seed), 5)
    tokens = noise(streams_of[0], (TOKENS, D), 1.0, 6.0, ((0, 8), (1, 64)))
    gate_weight = noise(streams_of[1], (D, FF), D ** -0.5, 0.0625, ((0, 8), (1, 64)))
    up_weight = noise(streams_of[2], (D, FF), D ** -0.5, 0.0625, ((0, 8), (1, 64)))
    hidden_grad = noise(streams_of[3], (TOKENS, FF), 0.25, 1.5, ((0, 8), (1, 64)))
    return dict(tokens=tokens, gate_weight=gate_weight, up_weight=up_weight, hidden_grad=hidden_grad)


def reference(tokens, gate_weight, up_weight, hidden_grad):
    gate_sum = jnp.dot(tokens, gate_weight, preferred_element_type=jnp.float32)
    up_sum = jnp.dot(tokens, up_weight, preferred_element_type=jnp.float32)
    sigmoid_gate = jax.nn.sigmoid(gate_sum)
    activated = gate_sum * sigmoid_gate
    hidden = (activated * up_sum).astype(jnp.bfloat16)
    upstream = hidden_grad.astype(jnp.float32)
    gate_grad = (upstream * up_sum * sigmoid_gate * (1.0 + gate_sum * (1.0 - sigmoid_gate))).astype(jnp.bfloat16)
    up_grad = (upstream * activated).astype(jnp.bfloat16)
    contract_last = (((1,), (1,)), ((), ()))
    input_grad = lax.dot_general(gate_grad, gate_weight, contract_last, preferred_element_type=jnp.float32)
    input_grad = input_grad + lax.dot_general(up_grad, up_weight, contract_last, preferred_element_type=jnp.float32)
    contract_rows = (((0,), (0,)), ((), ()))
    gate_wgrad = lax.dot_general(tokens, gate_grad, contract_rows, preferred_element_type=jnp.float32)
    up_wgrad = lax.dot_general(tokens, up_grad, contract_rows, preferred_element_type=jnp.float32)
    return (hidden, input_grad.astype(jnp.bfloat16), gate_wgrad.astype(jnp.bfloat16), up_wgrad.astype(jnp.bfloat16))
```

```python
import jax
import jax.numpy as jnp
from jax import lax
from jax.sharding import Mesh, PartitionSpec as P

PLANE = ("zl", "x", "zh")
F32 = jnp.float32
BF16 = jnp.bfloat16


def regroup():
    pairs = []
    for zl in range(4):
        for co in range(2):
            for c in range(2):
                for a in range(4):
                    work = (zl * 2 + co) * 8 + 4 * c + a
                    home = (a * 2 + co) * 8 + 2 * zl + (co ^ c)
                    pairs.append((work, home))
    return pairs


def swap_cores(value):
    return lax.ppermute(value, "co", [(0, 1), (1, 0)])


def spread(value, axes, count):
    return lax.all_to_all(jnp.tile(value, (count, 1)), axes, 0, 0, tiled=True)


def body(tokens, gate_weight, up_weight, hidden_grad):
    to_home = regroup()
    to_work = [(home, work) for work, home in to_home]
    tiles = spread(tokens, PLANE, 32)
    own_weight = jnp.concatenate([gate_weight, up_weight], axis=1)
    other_weight = swap_cores(own_weight)
    upstream = lax.ppermute(hidden_grad, ("zl", "co", "y"), to_work)
    rows = tiles.reshape(4, 8, 128, 128).transpose(0, 2, 1, 3).reshape(512, 1024)
    own_part = jnp.dot(rows, own_weight, preferred_element_type=F32).astype(BF16)
    other_part = jnp.dot(rows, other_weight, preferred_element_type=F32).astype(BF16)
    parts = jnp.concatenate([own_part, other_part], axis=0)
    parts = lax.all_to_all(parts, "y", 0, 0, tiled=True)
    other_rows = swap_cores(rows)
    sums = jnp.sum(parts.reshape(8, 128, 512).astype(F32), axis=0)
    gate_sum, up_sum = sums[:, :256], sums[:, 256:]
    sigmoid_gate = jax.nn.sigmoid(gate_sum)
    activated = gate_sum * sigmoid_gate
    hidden = (activated * up_sum).astype(BF16)
    upstream = upstream.astype(F32)
    gate_grad = upstream * up_sum * sigmoid_gate * (1.0 + gate_sum * (1.0 - sigmoid_gate))
    up_grad = upstream * activated
    grads = jnp.concatenate([gate_grad.astype(BF16), up_grad.astype(BF16)], axis=1)
    grads = spread(grads, "y", 8)
    own_grads, other_grads = grads[:512], grads[512:]
    contract_last = (((1,), (1,)), ((), ()))
    input_part = lax.dot_general(own_grads, own_weight, contract_last, preferred_element_type=F32)
    input_part += lax.dot_general(
        other_grads, other_weight, contract_last, preferred_element_type=F32
    )
    blocks = input_part.astype(BF16).reshape(4, 128, 8, 128).transpose(0, 2, 1, 3)
    blocks = lax.all_to_all(blocks.reshape(32 * 128, 128), PLANE, 0, 0, tiled=True)
    hidden = lax.ppermute(hidden, ("zl", "co", "y"), to_home)
    received_grads = swap_cores(other_grads)
    contract_rows = (((0,), (0,)), ((), ()))
    wgrad = lax.dot_general(rows, own_grads, contract_rows, preferred_element_type=F32)
    wgrad += lax.dot_general(other_rows, received_grads, contract_rows, preferred_element_type=F32)
    wgrad = wgrad.astype(BF16)
    input_grad = jnp.sum(blocks.reshape(32, 128, 128).astype(F32), axis=0).astype(BF16)
    return hidden, input_grad, wgrad[:, :256], wgrad[:, 256:]


def solution(mesh):
    fine = Mesh(mesh.devices.reshape(4, 2, 4, 2, 8), ("zl", "co", "x", "zh", "y"))
    gx, gy, gz = ("zl", "co"), ("x", "zh"), ("y",)
    in_specs = (P(gx, gz + gy), P(gz, gy + gx), P(gz, gy + gx), P(gx, gy + gz))
    out_specs = (P(gx, gy + gz), P(gx, gz + gy), P(gz, gy + gx), P(gz, gy + gx))
    return jax.shard_map(body, mesh=fine, in_specs=in_specs, out_specs=out_specs, check_vma=False)
```

```python
import jax
import jax.numpy as jnp
from jax import lax
from jax.sharding import Mesh, PartitionSpec as P

PLANE = ("x", "zl", "zh")
F32 = jnp.float32
BF16 = jnp.bfloat16
LAST = (((1,), (1,)), ((), ()))
ROWS = (((0,), (0,)), ((), ()))


def regroup():
    pairs = []
    for zl in range(4):
        for co in range(2):
            for q in range(4):
                for p in range(2):
                    work = (zl * 2 + co) * 8 + 2 * q + p
                    home = (q * 2 + co) * 8 + 2 * zl + p
                    pairs.append((work, home))
    return pairs


def swap_cores(value):
    return lax.ppermute(value, "co", [(0, 1), (1, 0)])


def swap_pair(value):
    return lax.ppermute(value, "yp", [(0, 1), (1, 0)])


def body(tokens, gate_weight, up_weight, hidden_grad):
    core, side = lax.axis_index("co"), lax.axis_index("yp")
    low, own_first = side == 0, side == core
    perm = regroup()
    everyone = ("zl", "co", "yq", "yp")

    def split(value):
        return jnp.where(low, value[:64], value[64:]), jnp.where(low, value[64:], value[:64])

    def join(kept, received):
        return jnp.where(
            low, jnp.concatenate([kept, received]), jnp.concatenate([received, kept])
        )

    kept, sent = split(tokens)
    pair_tokens = jnp.concatenate([kept, swap_pair(sent)], axis=1)
    tiles = lax.all_to_all(jnp.tile(pair_tokens, (32, 1)), PLANE, 0, 0, tiled=True)
    own = jnp.concatenate([gate_weight, up_weight], axis=1)
    own_pair = swap_pair(own)
    other = swap_cores(own)
    other_pair = swap_cores(own_pair)
    upstream = lax.ppermute(hidden_grad, everyone, [(home, work) for work, home in perm])
    kept, sent = split(upstream)
    received = swap_pair(sent)
    upstream = jnp.where(
        own_first,
        jnp.concatenate([kept, received], axis=1),
        jnp.concatenate([received, kept], axis=1),
    ).astype(F32)

    rows = tiles.reshape(4, 4, 2, 64, 2, 128).transpose(1, 3, 4, 0, 2, 5).reshape(256, 2048)
    near_rows, far_rows = rows[:, :1024], rows[:, 1024:]

    def forward(near, far):
        return (
            jnp.dot(near_rows, near, preferred_element_type=F32)
            + jnp.dot(far_rows, far, preferred_element_type=F32)
        ).astype(BF16)

    parts = jnp.concatenate([forward(own, own_pair), forward(other, other_pair)], axis=1)
    parts = lax.all_to_all(parts, "yq", 0, 0, tiled=True)
    sums = jnp.sum(parts.reshape(4, 64, 1024).astype(F32), axis=0)
    gate_sum = jnp.concatenate([sums[:, :256], sums[:, 512:768]], axis=1)
    up_sum = jnp.concatenate([sums[:, 256:512], sums[:, 768:]], axis=1)
    sigmoid_gate = jax.nn.sigmoid(gate_sum)
    activated = gate_sum * sigmoid_gate
    hidden = (activated * up_sum).astype(BF16)
    gate_grad = upstream * up_sum * sigmoid_gate * (1.0 + gate_sum * (1.0 - sigmoid_gate))
    up_grad = upstream * activated
    gate_grad, up_grad = gate_grad.astype(BF16), up_grad.astype(BF16)
    grads = jnp.concatenate(
        [gate_grad[:, :256], up_grad[:, :256], gate_grad[:, 256:], up_grad[:, 256:]], axis=1
    )
    grads = lax.all_to_all(jnp.tile(grads, (4, 1)), "yq", 0, 0, tiled=True)
    own_grads, other_grads = grads[:, :512], grads[:, 512:]

    def backward(mine, others):
        return (
            lax.dot_general(own_grads, mine, LAST, preferred_element_type=F32)
            + lax.dot_general(other_grads, others, LAST, preferred_element_type=F32)
        ).astype(BF16)

    block = jnp.stack([backward(own, other), backward(own_pair, other_pair)])
    block = block.reshape(2, 4, 64, 4, 2, 128).transpose(3, 1, 4, 2, 0, 5).reshape(32 * 64, 256)
    block = lax.all_to_all(block, PLANE, 0, 0, tiled=True)

    kept = jnp.where(own_first, hidden[:, :256], hidden[:, 256:])
    sent = jnp.where(own_first, hidden[:, 256:], hidden[:, :256])
    hidden = lax.ppermute(join(kept, swap_pair(sent)), everyone, perm)

    pair_rows, pair_grads = swap_pair(far_rows), swap_pair(grads)
    mine_rows = jnp.concatenate([near_rows, pair_rows])
    mine_grads = jnp.concatenate([own_grads, pair_grads[:, :512]])
    their_grads = jnp.concatenate([other_grads, pair_grads[:, 512:]])
    wgrad = lax.dot_general(mine_rows, mine_grads, ROWS, preferred_element_type=F32)
    wgrad += lax.dot_general(
        swap_cores(mine_rows), swap_cores(their_grads), ROWS, preferred_element_type=F32
    )
    wgrad = wgrad.astype(BF16)
    block = jnp.sum(block.reshape(32, 64, 256).astype(F32), axis=0).astype(BF16)
    input_grad = join(block[:, :128], swap_pair(block[:, 128:]))
    return hidden, input_grad, wgrad[:, :256], wgrad[:, 256:]


def solution(mesh):
    axes = ("zl", "co", "x", "zh", "yq", "yp")
    fine = Mesh(mesh.devices.reshape(4, 2, 4, 2, 4, 2), axes)
    gx, gy, gz = ("zl", "co"), ("x", "zh"), ("yq", "yp")
    in_specs = (P(gx, gz + gy), P(gz, gy + gx), P(gz, gy + gx), P(gx, gy + gz))
    out_specs = (P(gx, gy + gz), P(gx, gz + gy), P(gz, gy + gx), P(gz, gy + gx))
    return jax.shard_map(body, mesh=fine, in_specs=in_specs, out_specs=out_specs, check_vma=False)
```

```python
import jax
import jax.numpy as jnp
from jax import lax
from jax.experimental import pallas as pl
from jax.experimental.pallas import tpu as pltpu
from jax.sharding import Mesh, PartitionSpec as P

PLANE = ("x", "zl", "zh")
F32 = jnp.float32
BF16 = jnp.bfloat16
LAST = (((1,), (1,)), ((), ()))
ROWS = (((0,), (0,)), ((), ()))


def regroup():
    pairs = []
    for zl in range(4):
        for co in range(2):
            for q in range(4):
                for p in range(2):
                    work = (zl * 2 + co) * 8 + 2 * q + p
                    home = (q * 2 + co) * 8 + 2 * zl + p
                    pairs.append((work, home))
    return pairs


def swap_cores(value):
    return lax.ppermute(value, "co", [(0, 1), (1, 0)])


def swap_pair(value):
    return lax.ppermute(value, "yp", [(0, 1), (1, 0)])


def forward_kernel(side_ref, tiles, own, own_pair, other, other_pair, parts, near, far):
    side = side_ref[0]
    for x in range(4):
        for zl in range(4):
            for zh in range(2):
                row, column = slice(64 * zl, 64 * zl + 64), slice(128 * (2 * x + zh), 128 * (2 * x + zh + 1))
                near[row, column] = tiles[x, zl, zh, side]
                far[row, column] = tiles[x, zl, zh, 1 - side]
    for at, (first, second) in enumerate(((own, own_pair), (other, other_pair))):
        total = jnp.dot(near[...], first[...], preferred_element_type=F32)
        total += jnp.dot(far[...], second[...], preferred_element_type=F32)
        parts[:, 512 * at : 512 * (at + 1)] = total.astype(BF16)


def backward_kernel(side_ref, grads, own, own_pair, other, other_pair, blocks):
    side = side_ref[0]
    for place, first, second in ((side, own, other), (1 - side, own_pair, other_pair)):
        for x in range(4):
            rows = slice(256 * x, 256 * (x + 1))
            total = lax.dot_general(grads[:, :512], first[rows], LAST, preferred_element_type=F32)
            total += lax.dot_general(grads[:, 512:], second[rows], LAST, preferred_element_type=F32)
            total = total.astype(BF16)
            for zl in range(4):
                for zh in range(2):
                    tile = total[64 * zl : 64 * zl + 64, 128 * zh : 128 * zh + 128]
                    blocks[x, zl, zh, place] = tile


def call(kernel, out_shapes, inputs):
    vmem = pl.BlockSpec(memory_space=pltpu.VMEM)
    return pl.pallas_call(
        kernel,
        out_shape=[jax.ShapeDtypeStruct(shape, BF16) for shape in out_shapes],
        in_specs=[pl.BlockSpec(memory_space=pltpu.SMEM)] + [vmem] * (len(inputs) - 1),
        out_specs=[vmem] * len(out_shapes),
        compiler_params=pltpu.CompilerParams(vmem_limit_bytes=40 * 1024 * 1024),
    )(*inputs)


def body(tokens, gate_weight, up_weight, hidden_grad):
    core, side = lax.axis_index("co"), lax.axis_index("yp")
    low, own_first = side == 0, side == core
    side_word = side.astype(jnp.int32).reshape(1)
    perm = regroup()
    everyone = ("zl", "co", "yq", "yp")

    copies, gate_weight, up_weight, hidden_grad = lax.optimization_barrier(
        (jnp.tile(tokens, (32, 1)), gate_weight, up_weight, hidden_grad)
    )
    tiles = lax.all_to_all(copies, PLANE + ("yp",), 0, 0, tiled=True)
    own = jnp.concatenate([gate_weight, up_weight], axis=1)
    own_pair = swap_pair(own)
    other = swap_cores(own)
    other_pair = swap_cores(own_pair)
    weights = (own, own_pair, other, other_pair)
    upstream = lax.ppermute(hidden_grad, everyone, [(home, work) for work, home in perm])
    kept = jnp.where(low, upstream[:64], upstream[64:])
    received = swap_pair(jnp.where(low, upstream[64:], upstream[:64]))
    upstream = jnp.where(
        own_first,
        jnp.concatenate([kept, received], axis=1),
        jnp.concatenate([received, kept], axis=1),
    ).astype(F32)

    parts, near_rows, far_rows = call(
        forward_kernel,
        [(256, 1024)] * 3,
        (side_word, tiles.reshape(4, 4, 2, 2, 64, 128)) + weights,
    )
    parts = lax.all_to_all(parts, "yq", 0, 0, tiled=True)
    sums = jnp.sum(parts.reshape(4, 64, 1024).astype(F32), axis=0)
    gate_sum = jnp.concatenate([sums[:, :256], sums[:, 512:768]], axis=1)
    up_sum = jnp.concatenate([sums[:, 256:512], sums[:, 768:]], axis=1)
    sigmoid_gate = jax.nn.sigmoid(gate_sum)
    activated = gate_sum * sigmoid_gate
    hidden = (activated * up_sum).astype(BF16)
    gate_grad = upstream * up_sum * sigmoid_gate * (1.0 + gate_sum * (1.0 - sigmoid_gate))
    up_grad = upstream * activated
    gate_grad, up_grad = gate_grad.astype(BF16), up_grad.astype(BF16)
    grads = jnp.concatenate(
        [gate_grad[:, :256], up_grad[:, :256], gate_grad[:, 256:], up_grad[:, 256:]], axis=1
    )
    grads = lax.all_to_all(jnp.tile(grads, (4, 1)), "yq", 0, 0, tiled=True)

    grads, far_rows = lax.optimization_barrier((grads, far_rows))
    (blocks,) = call(backward_kernel, [(4, 4, 2, 2, 64, 128)], (side_word, grads) + weights)
    blocks = lax.all_to_all(
        blocks.reshape(64 * 64, 128), PLANE + ("yp",), 0, 0, tiled=True
    )

    kept = jnp.where(own_first, hidden[:, :256], hidden[:, 256:])
    received = swap_pair(jnp.where(own_first, hidden[:, 256:], hidden[:, :256]))
    hidden = jnp.where(low, jnp.concatenate([kept, received]), jnp.concatenate([received, kept]))
    hidden = lax.ppermute(hidden, everyone, perm)

    pair_grads = swap_pair(grads)
    pair_rows = swap_pair(far_rows)
    wgrad = sum(
        lax.dot_general(left, right, ROWS, preferred_element_type=F32)
        for left, right in (
            (near_rows, grads[:, :512]),
            (swap_cores(near_rows), swap_cores(grads[:, 512:])),
            (pair_rows, pair_grads[:, :512]),
            (swap_cores(pair_rows), swap_cores(pair_grads[:, 512:])),
        )
    )
    wgrad = wgrad.astype(BF16)
    input_grad = jnp.sum(blocks.reshape(32, 128, 128).astype(F32), axis=0).astype(BF16)
    return hidden, input_grad, wgrad[:, :256], wgrad[:, 256:]


def solution(mesh):
    axes = ("zl", "co", "x", "zh", "yq", "yp")
    fine = Mesh(mesh.devices.reshape(4, 2, 4, 2, 4, 2), axes)
    gx, gy, gz = ("zl", "co"), ("x", "zh"), ("yq", "yp")
    in_specs = (P(gx, gz + gy), P(gz, gy + gx), P(gz, gy + gx), P(gx, gy + gz))
    out_specs = (P(gx, gy + gz), P(gx, gz + gy), P(gz, gy + gx), P(gz, gy + gx))
    return jax.shard_map(body, mesh=fine, in_specs=in_specs, out_specs=out_specs, check_vma=False)
```

```python
import jax
import jax.numpy as jnp
from jax import lax
from jax.experimental import pallas as pl
from jax.experimental.pallas import tpu as pltpu
from jax.sharding import Mesh, PartitionSpec as P

PLANE = ("x", "zl", "zh")
F32 = jnp.float32
BF16 = jnp.bfloat16
LAST = (((1,), (1,)), ((), ()))
ROWS = (((0,), (0,)), ((), ()))


def regroup():
    pairs = []
    for zl in range(4):
        for co in range(2):
            for c in range(2):
                for a in range(4):
                    work = (zl * 2 + co) * 8 + 4 * c + a
                    home = (a * 2 + co) * 8 + 2 * zl + (co ^ c)
                    pairs.append((work, home))
    return pairs


def swap_cores(value):
    return lax.ppermute(value, "co", [(0, 1), (1, 0)])


def spread(value, axes, count):
    return lax.all_to_all(jnp.tile(value, (count, 1)), axes, 0, 0, tiled=True)


def forward_kernel(tiles, own_gate, own_up, other_gate, other_up, parts, rows):
    for x in range(4):
        for zl in range(4):
            for zh in range(2):
                column = 128 * (2 * x + zh)
                rows[128 * zl : 128 * zl + 128, column : column + 128] = tiles[x, zl, zh]
    for at, weight in enumerate((own_gate, own_up, other_gate, other_up)):
        sums = jnp.dot(rows[...], weight[...], preferred_element_type=F32)
        row, column = 512 * (at // 2), 256 * (at % 2)
        parts[row : row + 512, column : column + 256] = sums.astype(BF16)


def backward_kernel(grads, own_gate, own_up, other_gate, other_up, blocks):
    for x in range(4):
        rows = slice(256 * x, 256 * x + 256)
        sums = 0.0
        for at, weight in enumerate((own_gate, own_up, other_gate, other_up)):
            row, column = 512 * (at // 2), 256 * (at % 2)
            sums += lax.dot_general(
                grads[row : row + 512, column : column + 256],
                weight[rows],
                LAST,
                preferred_element_type=F32,
            )
        sums = sums.astype(BF16)
        for zl in range(4):
            for zh in range(2):
                blocks[x, zl, zh] = sums[128 * zl : 128 * zl + 128, 128 * zh : 128 * zh + 128]


def call(kernel, outputs, inputs):
    vmem = pl.BlockSpec(memory_space=pltpu.VMEM)
    return pl.pallas_call(
        kernel,
        out_shape=[jax.ShapeDtypeStruct(shape, BF16) for shape in outputs],
        in_specs=[vmem] * len(inputs),
        out_specs=[vmem] * len(outputs),
        compiler_params=pltpu.CompilerParams(vmem_limit_bytes=40 * 1024 * 1024),
    )(*inputs)


def gather_rows(tokens):
    return spread(tokens, PLANE, 32)


def body(tokens, gate_weight, up_weight, hidden_grad):
    to_home = regroup()
    to_work = [(home, work) for work, home in to_home]
    tiles = gather_rows(tokens)
    weights = (gate_weight, up_weight, swap_cores(gate_weight), swap_cores(up_weight))
    upstream = lax.ppermute(hidden_grad, ("zl", "co", "y"), to_work)
    parts, rows = call(
        forward_kernel,
        [(1024, 512), (512, 1024)],
        (tiles.reshape(4, 4, 2, 128, 128),) + weights,
    )
    parts = lax.all_to_all(parts, "y", 0, 0, tiled=True)
    sums = jnp.sum(parts.reshape(8, 128, 512).astype(F32), axis=0)
    gate_sum, up_sum = sums[:, :256], sums[:, 256:]
    sigmoid_gate = jax.nn.sigmoid(gate_sum)
    activated = gate_sum * sigmoid_gate
    hidden = (activated * up_sum).astype(BF16)
    upstream = upstream.astype(F32)
    gate_grad = upstream * up_sum * sigmoid_gate * (1.0 + gate_sum * (1.0 - sigmoid_gate))
    up_grad = upstream * activated
    mine = jnp.concatenate([gate_grad.astype(BF16), up_grad.astype(BF16)], axis=1)
    grads = spread(mine, "y", 8)
    (blocks,) = call(backward_kernel, [(4, 4, 2, 128, 128)], (grads,) + weights)
    blocks, grads, rows = lax.optimization_barrier((blocks, grads, rows))
    blocks = lax.all_to_all(blocks.reshape(32 * 128, 128), PLANE, 0, 0, tiled=True)
    received_grads = swap_cores(grads[512:])
    other_rows = swap_cores(rows)
    hidden = lax.ppermute(hidden, ("zl", "co", "y"), to_home)
    wgrad = lax.dot_general(rows, grads[:512], ROWS, preferred_element_type=F32)
    wgrad += lax.dot_general(other_rows, received_grads, ROWS, preferred_element_type=F32)
    wgrad = wgrad.astype(BF16)
    input_grad = jnp.sum(blocks.reshape(32, 128, 128).astype(F32), axis=0).astype(BF16)
    return hidden, input_grad, wgrad[:, :256], wgrad[:, 256:]


def solution(mesh):
    fine = Mesh(mesh.devices.reshape(4, 2, 4, 2, 8), ("zl", "co", "x", "zh", "y"))
    gx, gy, gz = ("zl", "co"), ("x", "zh"), ("y",)
    in_specs = (P(gx, gz + gy), P(gz, gy + gx), P(gz, gy + gx), P(gx, gy + gz))
    out_specs = (P(gx, gy + gz), P(gx, gz + gy), P(gz, gy + gx), P(gz, gy + gx))
    return jax.shard_map(body, mesh=fine, in_specs=in_specs, out_specs=out_specs, check_vma=False)
```

```python
import jax
import jax.numpy as jnp
from jax import lax
from jax.experimental import pallas as pl
from jax.experimental.pallas import tpu as pltpu
from jax.sharding import Mesh, PartitionSpec as P

RING = ("zl", "zh")
F32 = jnp.float32
BF16 = jnp.bfloat16
LAST = (((1,), (1,)), ((), ()))
ROWS = (((0,), (0,)), ((), ()))


def regroup():
    pairs = []
    for zl in range(4):
        for co in range(2):
            for c in range(2):
                for a in range(4):
                    work = (zl * 2 + co) * 8 + 4 * c + a
                    home = (a * 2 + co) * 8 + 2 * zl + (co ^ c)
                    pairs.append((work, home))
    return pairs


def swap_cores(value):
    return lax.ppermute(value, "co", [(0, 1), (1, 0)])


def spread(value, axes, count):
    return lax.all_to_all(jnp.tile(value, (count, 1)), axes, 0, 0, tiled=True)


def forward_kernel(tiles, own_gate, own_up, other_gate, other_up, parts, rows):
    for x in range(4):
        for zl in range(4):
            for zh in range(2):
                column = 128 * (2 * x + zh)
                rows[128 * zl : 128 * zl + 128, column : column + 128] = tiles[x, zl, zh]
    for at, weight in enumerate((own_gate, own_up, other_gate, other_up)):
        sums = jnp.dot(rows[...], weight[...], preferred_element_type=F32)
        row, column = 512 * (at // 2), 256 * (at % 2)
        parts[row : row + 512, column : column + 256] = sums.astype(BF16)


def backward_kernel(grads, own_gate, own_up, other_gate, other_up, blocks):
    for x in range(4):
        rows = slice(256 * x, 256 * x + 256)
        sums = 0.0
        for at, weight in enumerate((own_gate, own_up, other_gate, other_up)):
            row, column = 512 * (at // 2), 256 * (at % 2)
            sums += lax.dot_general(
                grads[row : row + 512, column : column + 256],
                weight[rows],
                LAST,
                preferred_element_type=F32,
            )
        sums = sums.astype(BF16)
        for zl in range(4):
            for zh in range(2):
                blocks[x, zl, zh] = sums[128 * zl : 128 * zl + 128, 128 * zh : 128 * zh + 128]


def call(kernel, outputs, inputs):
    vmem = pl.BlockSpec(memory_space=pltpu.VMEM)
    return pl.pallas_call(
        kernel,
        out_shape=[jax.ShapeDtypeStruct(shape, BF16) for shape in outputs],
        in_specs=[vmem] * len(inputs),
        out_specs=[vmem] * len(outputs),
        compiler_params=pltpu.CompilerParams(vmem_limit_bytes=40 * 1024 * 1024),
    )(*inputs)


def gather_rows(tokens):
    return spread(spread(tokens, RING, 8), "x", 4)


def body(tokens, gate_weight, up_weight, hidden_grad):
    to_home = regroup()
    to_work = [(home, work) for work, home in to_home]
    tiles = gather_rows(tokens)
    weights = (gate_weight, up_weight, swap_cores(gate_weight), swap_cores(up_weight))
    upstream = lax.ppermute(hidden_grad, ("zl", "co", "y"), to_work)
    tiles, upstream = lax.optimization_barrier((tiles, upstream))
    parts, rows = call(
        forward_kernel,
        [(1024, 512), (512, 1024)],
        (tiles.reshape(4, 4, 2, 128, 128),) + weights,
    )
    parts = lax.all_to_all(parts, "y", 0, 0, tiled=True)
    sums = jnp.sum(parts.reshape(8, 128, 512).astype(F32), axis=0)
    gate_sum, up_sum = sums[:, :256], sums[:, 256:]
    sigmoid_gate = jax.nn.sigmoid(gate_sum)
    activated = gate_sum * sigmoid_gate
    hidden = (activated * up_sum).astype(BF16)
    upstream = upstream.astype(F32)
    gate_grad = upstream * up_sum * sigmoid_gate * (1.0 + gate_sum * (1.0 - sigmoid_gate))
    up_grad = upstream * activated
    mine = jnp.concatenate([gate_grad.astype(BF16), up_grad.astype(BF16)], axis=1)
    grads = spread(mine, "y", 8)
    (blocks,) = call(backward_kernel, [(4, 4, 2, 128, 128)], (grads,) + weights)
    blocks, grads, rows = lax.optimization_barrier((blocks, grads, rows))
    blocks = lax.all_to_all(blocks.reshape(32 * 128, 128), "x", 0, 0, tiled=True)
    blocks = jnp.sum(blocks.reshape(4, 8 * 128, 128).astype(F32), axis=0).astype(BF16)
    blocks = lax.all_to_all(blocks, RING, 0, 0, tiled=True)
    received_grads = swap_cores(grads[512:])
    other_rows = swap_cores(rows)
    hidden = lax.ppermute(hidden, ("zl", "co", "y"), to_home)
    wgrad = lax.dot_general(rows, grads[:512], ROWS, preferred_element_type=F32)
    wgrad += lax.dot_general(other_rows, received_grads, ROWS, preferred_element_type=F32)
    wgrad = wgrad.astype(BF16)
    input_grad = jnp.sum(blocks.reshape(8, 128, 128).astype(F32), axis=0).astype(BF16)
    return hidden, input_grad, wgrad[:, :256], wgrad[:, 256:]


def solution(mesh):
    fine = Mesh(mesh.devices.reshape(4, 2, 4, 2, 8), ("zl", "co", "x", "zh", "y"))
    gx, gy, gz = ("zl", "co"), ("x", "zh"), ("y",)
    in_specs = (P(gx, gz + gy), P(gz, gy + gx), P(gz, gy + gx), P(gx, gy + gz))
    out_specs = (P(gx, gy + gz), P(gx, gz + gy), P(gz, gy + gx), P(gz, gy + gx))
    return jax.shard_map(body, mesh=fine, in_specs=in_specs, out_specs=out_specs, check_vma=False)
```

```python
import jax
import jax.numpy as jnp
from jax import lax
from jax.experimental import pallas as pl
from jax.experimental.pallas import tpu as pltpu
from jax.sharding import Mesh, PartitionSpec as P

RING = ("zl", "zh")
F32 = jnp.float32
BF16 = jnp.bfloat16
LAST = (((1,), (1,)), ((), ()))
ROWS = (((0,), (0,)), ((), ()))


def regroup():
    pairs = []
    for zl in range(4):
        for co in range(2):
            for c in range(2):
                for a in range(4):
                    work = (zl * 2 + co) * 8 + 4 * c + a
                    home = (a * 2 + co) * 8 + 2 * zl + (co ^ c)
                    pairs.append((work, home))
    return pairs


def swap_cores(value):
    return lax.ppermute(value, "co", [(0, 1), (1, 0)])


def spread(value, axes, count):
    return lax.all_to_all(jnp.tile(value, (count, 1)), axes, 0, 0, tiled=True)


def forward_kernel(tiles, own_gate, own_up, other_gate, other_up, parts, rows):
    for x in range(4):
        for zl in range(4):
            for zh in range(2):
                column = 128 * (2 * x + zh)
                rows[128 * zl : 128 * zl + 128, column : column + 128] = tiles[x, zl, zh]
    for at, weight in enumerate((own_gate, own_up, other_gate, other_up)):
        sums = jnp.dot(rows[...], weight[...], preferred_element_type=F32)
        row, column = 512 * (at // 2), 256 * (at % 2)
        parts[row : row + 512, column : column + 256] = sums.astype(BF16)


def backward_kernel(grads, own_gate, own_up, other_gate, other_up, blocks):
    for x in range(4):
        rows = slice(256 * x, 256 * x + 256)
        sums = 0.0
        for at, weight in enumerate((own_gate, own_up, other_gate, other_up)):
            row, column = 512 * (at // 2), 256 * (at % 2)
            sums += lax.dot_general(
                grads[row : row + 512, column : column + 256],
                weight[rows],
                LAST,
                preferred_element_type=F32,
            )
        sums = sums.astype(BF16)
        for zl in range(4):
            for zh in range(2):
                blocks[x, zl, zh] = sums[128 * zl : 128 * zl + 128, 128 * zh : 128 * zh + 128]


def call(kernel, outputs, inputs):
    vmem = pl.BlockSpec(memory_space=pltpu.VMEM)
    return pl.pallas_call(
        kernel,
        out_shape=[jax.ShapeDtypeStruct(shape, BF16) for shape in outputs],
        in_specs=[vmem] * len(inputs),
        out_specs=[vmem] * len(outputs),
        compiler_params=pltpu.CompilerParams(vmem_limit_bytes=40 * 1024 * 1024),
    )(*inputs)


def gather_rows(tokens):
    return spread(spread(tokens, RING, 8), "x", 4)


def body(tokens, gate_weight, up_weight, hidden_grad):
    to_home = regroup()
    to_work = [(home, work) for work, home in to_home]
    tiles = gather_rows(tokens)
    weights = (gate_weight, up_weight, swap_cores(gate_weight), swap_cores(up_weight))
    upstream = lax.ppermute(hidden_grad, ("zl", "co", "y"), to_work)
    tiles, upstream = lax.optimization_barrier((tiles, upstream))
    parts, rows = call(
        forward_kernel,
        [(1024, 512), (512, 1024)],
        (tiles.reshape(4, 4, 2, 128, 128),) + weights,
    )
    parts = lax.all_to_all(parts, "y", 0, 0, tiled=True)
    sums = jnp.sum(parts.reshape(8, 128, 512).astype(F32), axis=0)
    gate_sum, up_sum = sums[:, :256], sums[:, 256:]
    sigmoid_gate = jax.nn.sigmoid(gate_sum)
    activated = gate_sum * sigmoid_gate
    hidden = (activated * up_sum).astype(BF16)
    upstream = upstream.astype(F32)
    gate_grad = upstream * up_sum * sigmoid_gate * (1.0 + gate_sum * (1.0 - sigmoid_gate))
    up_grad = upstream * activated
    mine = jnp.concatenate([gate_grad.astype(BF16), up_grad.astype(BF16)], axis=1)
    mine, rows = lax.optimization_barrier((mine, rows))
    grads = spread(mine, "y", 8)
    grads, other_rows = lax.optimization_barrier((grads, swap_cores(rows)))
    (blocks,) = call(backward_kernel, [(4, 4, 2, 128, 128)], (grads,) + weights)
    blocks, grads, hidden = lax.optimization_barrier((blocks, grads, hidden))
    blocks = lax.all_to_all(blocks.reshape(32 * 128, 128), "x", 0, 0, tiled=True)
    blocks = jnp.sum(blocks.reshape(4, 8 * 128, 128).astype(F32), axis=0).astype(BF16)
    blocks = lax.all_to_all(blocks, RING, 0, 0, tiled=True)
    received_grads = swap_cores(grads[512:])
    hidden = lax.ppermute(hidden, ("zl", "co", "y"), to_home)
    wgrad = lax.dot_general(rows, grads[:512], ROWS, preferred_element_type=F32)
    wgrad += lax.dot_general(other_rows, received_grads, ROWS, preferred_element_type=F32)
    wgrad = wgrad.astype(BF16)
    input_grad = jnp.sum(blocks.reshape(8, 128, 128).astype(F32), axis=0).astype(BF16)
    return hidden, input_grad, wgrad[:, :256], wgrad[:, 256:]


def solution(mesh):
    fine = Mesh(mesh.devices.reshape(4, 2, 4, 2, 8), ("zl", "co", "x", "zh", "y"))
    gx, gy, gz = ("zl", "co"), ("x", "zh"), ("y",)
    in_specs = (P(gx, gz + gy), P(gz, gy + gx), P(gz, gy + gx), P(gx, gy + gz))
    out_specs = (P(gx, gy + gz), P(gx, gz + gy), P(gz, gy + gx), P(gz, gy + gx))
    return jax.shard_map(body, mesh=fine, in_specs=in_specs, out_specs=out_specs, check_vma=False)
```
